32 devices in a mesh: seq: 8 (over z, x), fsdp: 4 (over y, core).
Axes of the slice: x: 2, y: 2, z: 4, core: 2. Of those that a mesh axis runs over, the one named last changes fastest.
Arguments:
- projected: bfloat16 [3, 8192, 4096], P(None, 'fsdp', 'seq'), may hold values from -6 to 6
- short_weight: float32 [3, 8192, 3], P(None, 'fsdp'), may hold values from -3.5 to 3.5
- skip_weight: float32 [8192], P('fsdp'), may hold values from -4 to 4
- decay_rates: float32 [8192, 16], P('fsdp'), may hold values from 0.00012207031 to 0.05
- residues: float32 [8192, 16], P('fsdp'), may hold values from -1.5 to 1.5
Outputs:
- output: bfloat16 [8192, 4096], P('fsdp', 'seq')
The draws below stay inside these ranges and needn't reach their ends.
All inputs are finite; a program needn't handle non-finite values.
Results may differ from the reference program's by a relative error of at most 0.0058.
Values may be sent and summed in bfloat16 or wider, within the bound.
A program may use at most 128 MiB of HBM per device.

```python
import math
import jax
import jax.numpy as jnp
from jax import lax

D = 8192
ORDER = 16
KS = 3
TOKENS = 4096


def shard_levels(key, dims, pieces, low, high):
    def one(dim, shards_of):
        heights = jax.random.uniform(jax.random.fold_in(jax.random.fold_in(key, 6), dim), (shards_of,), jnp.float32, low / len(pieces), high / len(pieces))
        return jnp.repeat(jnp.exp(heights), dims[dim] // shards_of).reshape((-1,) + (1,) * (len(dims) - dim - 1))

    loudness = one(*pieces[0])
    for cut in pieces[1:]:
        loudness = loudness * one(*cut)
    return loudness


def noise(own_key, shape, deviation, most, cuts=(), kind=jnp.bfloat16):
    entries = jax.random.normal(own_key, shape, jnp.float32) * deviation
    if len(cuts) > 0:
        entries = shard_levels(own_key, shape, cuts, -0.22, 0.18) * entries
    return jnp.clip(entries, min=-most, max=most).astype(kind)


def setup_inputs(seed: int = 0) -> dict:
    seeds = jax.random.split(jax.random.key(seed), 6)
    return {
        "projected": noise(seeds[0], (3, D, TOKENS), 1.0, 6.0, ((1, 4), (2, 8))),
        "short_weight": noise(seeds[1], (3, D, KS), KS ** -0.5, 3.5, ((1, 4),), jnp.float32),
        "skip_weight": noise(seeds[2], (D,), 1.0, 4.0, ((0, 4),), jnp.float32),
        "decay_rates": jnp.clip(jnp.exp(math.log(0.05) - 6.015181 * jax.random.uniform(seeds[3], (D, ORDER), jnp.float32) ** shard_levels(seeds[3], (D, ORDER), ((0, 4),), -0.2, 0.2)), 0.00012207031, 0.05),
        "residues": noise(seeds[4], (D, ORDER), 0.25, 1.5, ((0, 4),), jnp.float32),
    }


def reference(projected, short_weight, skip_weight, decay_rates, residues):
    length = projected.shape[2]
    taps_count = short_weight.shape[2]
    group = math.gcd(D, 32)

    def one_group(number):
        first = (number * group).astype(jnp.int32)
        block = lax.dynamic_slice_in_dim(projected, first, group, 1).astype(jnp.float32)
        weights = lax.dynamic_slice_in_dim(short_weight, first, group, 1)
        padded = jnp.pad(block, ((0, 0), (0, 0), (taps_count - 1, 0)))
        feats = jnp.zeros_like(block)
        for lag in range(taps_count):
            begin = taps_count - 1 - lag
            feats = feats + weights[:, :, lag][:, :, None] * padded[:, :, begin:begin + length]
        mixed = (feats[1] * feats[2]).astype(jnp.bfloat16)
        mixed = lax.optimization_barrier(mixed)
        signal = mixed.astype(jnp.float32)
        decay_rate = lax.dynamic_slice_in_dim(decay_rates, first, group, 0)
        residue = lax.dynamic_slice_in_dim(residues, first, group, 0)
        offsets = jnp.arange(length, dtype=jnp.float32)
        scaled = residue * jnp.sqrt(2.0 * decay_rate)
        filt = lax.optimization_barrier(jnp.sum(scaled[:, :, None] * jnp.exp(-decay_rate[:, :, None] * offsets), axis=1))
        padded_len = 2 * length
        spectrum = jnp.fft.rfft(filt, padded_len) * jnp.fft.rfft(signal, padded_len)
        convolved = jnp.fft.irfft(spectrum, padded_len)[:, :length]
        gains = lax.dynamic_slice_in_dim(skip_weight, first, group, 0)
        summed = (convolved + gains[:, None] * signal).astype(jnp.bfloat16)
        summed = lax.optimization_barrier(summed)
        return (feats[0] * summed.astype(jnp.float32)).astype(jnp.bfloat16)
    result = lax.map(one_group, jnp.arange(D // group, dtype=jnp.int32))
    return result.reshape(D, length)
```

```python
import functools

import jax
import jax.numpy as jnp
import numpy as np
from jax import lax
from jax.experimental import pallas as pl
from jax.experimental.pallas import tpu as pltpu
from jax.sharding import PartitionSpec as P

BL = 128
NB = 16
HALF = 0.025


def split(m):
    hi = m.astype(jnp.bfloat16)
    return hi, (m - np.asarray(hi, np.float64)).astype(jnp.bfloat16)


@functools.cache
def tables():
    nodes = 64
    theta = (np.arange(nodes) + 0.5) * np.pi / nodes
    t = np.arange(BL + 1)
    f = np.exp(-HALF * (1 + np.cos(theta))[:, None] * t[None, :])
    psi = np.stack(
        [(2.0 if n else 1.0) / nodes * (np.cos(n * theta) @ f) for n in range(NB)]
    )
    half = BL // 2
    ang = np.pi * np.outer(np.arange(BL), 2 * np.arange(half) + 1) / BL
    c, s = np.cos(ang), np.sin(ang)
    z = np.zeros_like(c)
    fwd = np.block([[c, z, -s, z], [z, c, z, -s]])
    inv = np.block([[c, z, -s, z], [z, c, z, -s]]).T * (2.0 / BL)
    spec = np.concatenate([psi[:, :BL] @ c] * 2 + [-psi[:, :BL] @ s] * 2, axis=1)
    unit = np.concatenate([np.ones((1, BL)), np.zeros((1, BL))], axis=1)
    spec = np.concatenate([spec, unit, np.zeros((15, 2 * BL))], axis=0)
    rev = psi[:, BL - 1 :: -1][:, :BL]
    zr = np.zeros_like(rev)
    mom = np.block([[rev, zr], [zr, rev]])
    nxt = psi[:, 1 : BL + 1]
    car = np.block([[nxt, zr], [zr, nxt]])
    sh, sl = split(spec)
    mh, ml = split(mom)
    ch, cl = split(car)
    sel = np.zeros((8, 6 * 128))
    for i in range(3):
        sel[2 * i + 1, (2 * i) * 128] = 1
        sel[2 * i, (2 * i + 1) * 128] = 1
        sel[2 * i + 1, (2 * i + 1) * 128 + 1] = 1
    cat = lambda *a: np.concatenate(a, axis=0)
    b16 = lambda a: a.astype(jnp.bfloat16)
    return dict(
        fwd=b16(fwd), inv=b16(inv), spec=cat(sh, sh, sl), mom=cat(mh, ml),
        car=cat(ch, ch, cl), sel=b16(sel),
    )


def rowdot(a, b):
    return lax.dot_general(a, b, (((0,), (0,)), ((), ())), preferred_element_type=jnp.float32)


def three(m):
    hi = m.astype(jnp.bfloat16)
    lo = (m - hi.astype(jnp.float32)).astype(jnp.bfloat16)
    return jnp.concatenate([hi, lo, hi], axis=0)


def dot(a, b):
    return jnp.dot(a, b, preferred_element_type=jnp.float32)


def feat(x, w, h1, h2):
    lane = lax.broadcasted_iota(jnp.int32, (x.shape[0], 128), 1)
    w0, w1, w2 = (w[:, i : i + 1] for i in range(3))
    out = []
    for i in range(x.shape[1] // 128):
        c = x[:, i * 128 : (i + 1) * 128].astype(jnp.float32)
        r1, r2 = pltpu.roll(c, 1, 1), pltpu.roll(c, 2, 1)
        out.append(w0 * c + w1 * jnp.where(lane < 1, h1, r1) + w2 * jnp.where(lane < 2, h2, r2))
        h1, h2 = r1, r2
    return out


ROWS = 32


def front(p_ref, halo_ref, w_ref, cheb_ref, decay_ref, sel_ref, mom_ref,
          mixed_ref, ends_ref, last_ref, hr_ref):
    tile = p_ref.shape[1]
    hr_ref[...] = rowdot(halo_ref[...], sel_ref[...])

    @pl.loop(0, tile // ROWS)
    def _(r):
        rows = pl.ds(pl.multiple_of(r * ROWS, ROWS), ROWS)
        k = feat(p_ref[1, rows, :], w_ref[1, rows, :], hr_ref[rows, 256:384], hr_ref[rows, 384:512])
        v = feat(p_ref[2, rows, :], w_ref[2, rows, :], hr_ref[rows, 512:640], hr_ref[rows, 640:768])
        for i in range(len(k)):
            mixed_ref[rows, i * 128 : (i + 1) * 128] = (k[i] * v[i]).astype(jnp.bfloat16)

    step = jnp.exp(-BL * decay_ref[...])
    total = None
    for pair in range(p_ref.shape[2] // 256):
        m = lax.dot_general(
            mom_ref[...], mixed_ref[:, pair * 256 : (pair + 1) * 256],
            (((1,), (1,)), ((), ())), preferred_element_type=jnp.float32)
        m = m[:32] + m[32:]
        for b in range(2):
            e = cheb_ref[0:16] * m[b * 16 : b * 16 + 1]
            for n in range(1, NB):
                e = e + cheb_ref[n * 16 : n * 16 + 16] * m[b * 16 + n : b * 16 + n + 1]
            ends_ref[(pair * 2 + b) * 16 : (pair * 2 + b + 1) * 16] = e
            total = e if total is None else step * total + e
    last_ref[...] = total.astype(last_ref.dtype)


def back(q_ref, mixed_ref, halo_ref, w_ref, cheb_ref, decay_ref, weight_ref, skip_ref, ends_ref, init_ref,
         sel_ref, fwd_ref, inv_ref, spec_ref, car_ref,
         out_ref, hr_ref, h_ref, y_ref):
    tile = mixed_ref.shape[0]
    hr_ref[...] = rowdot(halo_ref[...], sel_ref[:, :256])
    step = jnp.exp(-BL * decay_ref[...])
    fold = 1.0 / (1.0 + step)
    weight = weight_ref[...]
    wv = weight * fold
    g = [jnp.sum(wv * cheb_ref[n * 16 : n * 16 + 16], axis=0, keepdims=True) for n in range(NB)]
    g = jnp.concatenate(g + [skip_ref[...], jnp.zeros((15, tile), jnp.float32)], axis=0)
    h_ref[...] = rowdot(three(g), spec_ref[...])
    state = init_ref[...]
    for pair in range(mixed_ref.shape[1] // 256):
        c = []
        for b in range(2):
            e = ends_ref[(pair * 2 + b) * 16 : (pair * 2 + b + 1) * 16]
            p = weight * (state + fold * e)
            state = step * state + e
            c += [jnp.sum(p * cheb_ref[n * 16 : n * 16 + 16], axis=0, keepdims=True) for n in range(NB)]
        cols = slice(pair * 256, pair * 256 + 256)
        carried = rowdot(three(jnp.concatenate(c, axis=0)), car_ref[...])
        x = dot(mixed_ref[:, cols], fwd_ref[...])
        xr, xi = x[:, :128], x[:, 128:]
        hr, hi = h_ref[:, :128], h_ref[:, 128:]
        y = jnp.concatenate([xr * hr - xi * hi, xr * hi + xi * hr], axis=1).astype(jnp.bfloat16)
        y_ref[:, cols] = (carried + dot(y, inv_ref[...])).astype(jnp.bfloat16)

    @pl.loop(0, tile // ROWS)
    def _(r):
        rows = pl.ds(pl.multiple_of(r * ROWS, ROWS), ROWS)
        q = feat(q_ref[0, rows, :], w_ref[0, rows, :], hr_ref[rows, 0:128], hr_ref[rows, 128:256])
        for i in range(len(q)):
            cols = slice(i * 128, i * 128 + 128)
            out_ref[rows, cols] = (q[i] * y_ref[rows, cols].astype(jnp.float32)).astype(jnp.bfloat16)


def shards(projected, short_weight, skip_weight, decay_rates, residues):
    channels, length = projected.shape[1:]
    n = lax.axis_size("seq")
    me = lax.axis_index("seq")
    tab = {k: jnp.asarray(v) for k, v in tables().items()}
    tile = min(256, channels)
    blocks = length // BL
    tail = jnp.swapaxes(projected[:, :, length - 2 :], 1, 2)
    halo = lax.ppermute(tail, "seq", [(i, i + 1) for i in range(n - 1)])
    halo = jnp.pad(halo.reshape(6, channels), ((0, 2), (0, 0)))
    decay = decay_rates.T
    weight = residues.T * jnp.sqrt(2.0 * decay)
    xi = decay / HALF - 1.0
    cheb = [jnp.ones_like(xi), xi]
    for _ in range(NB - 2):
        cheb.append(2.0 * xi * cheb[-1] - cheb[-2])
    cheb = jnp.concatenate(cheb, axis=0)

    full = lambda a: pl.BlockSpec(a.shape, lambda i: (0,) * a.ndim)
    lanes = lambda r: pl.BlockSpec((r, tile), lambda i: (0, i))
    rows = pl.BlockSpec((tile, length), lambda i: (i, 0))
    params = pltpu.CompilerParams(vmem_limit_bytes=40 * 2**20)
    pspec = pl.BlockSpec((3, tile, length), lambda i: (0, i, 0))
    qspec = pl.BlockSpec((1, tile, length), lambda i: (0, i, 0))
    wspec = pl.BlockSpec((3, tile, 3), lambda i: (0, i, 0))
    mixed, ends, last = pl.pallas_call(
        front,
        grid=(channels // tile,),
        in_specs=[pspec, lanes(8), wspec, lanes(NB * 16), lanes(16), full(tab["sel"]), full(tab["mom"])],
        out_specs=[rows, lanes(blocks * 16), lanes(16)],
        out_shape=[
            jax.ShapeDtypeStruct((channels, length), jnp.bfloat16),
            jax.ShapeDtypeStruct((blocks * 16, channels), jnp.float32),
            jax.ShapeDtypeStruct((16, channels), jnp.bfloat16),
        ],
        scratch_shapes=[pltpu.VMEM((tile, 768), jnp.float32)],
        compiler_params=params,
        name="front",
    )(projected, halo, short_weight, cheb, decay, tab["sel"], tab["mom"])
    every = lax.all_gather(last, "seq")
    whole_step = jnp.exp(-length * decay)
    init = jnp.zeros((16, channels), jnp.float32)
    for i in range(n - 1):
        init = jnp.where(i < me, whole_step * init + every[i].astype(jnp.float32), init)
    return pl.pallas_call(
        back,
        grid=(channels // tile,),
        in_specs=[qspec, rows, lanes(8), wspec, lanes(NB * 16), lanes(16), lanes(16), lanes(1),
                  lanes(blocks * 16), lanes(16)]
        + [full(tab[k]) for k in ("sel", "fwd", "inv", "spec", "car")],
        out_specs=rows,
        out_shape=jax.ShapeDtypeStruct((channels, length), jnp.bfloat16),
        scratch_shapes=[
            pltpu.VMEM((tile, 256), jnp.float32),
            pltpu.VMEM((tile, 256), jnp.float32),
            pltpu.VMEM((tile, length), jnp.bfloat16),
        ],
        compiler_params=params,
        name="back",
    )(projected, mixed, halo, short_weight, cheb, decay, weight, skip_weight[None], ends, init,
      *[tab[k] for k in ("sel", "fwd", "inv", "spec", "car")])


def solution(mesh):
    return jax.shard_map(
        shards,
        mesh=mesh,
        in_specs=(
            P(None, "fsdp", "seq"),
            P(None, "fsdp", None),
            P("fsdp"),
            P("fsdp", None),
            P("fsdp", None),
        ),
        out_specs=P("fsdp", "seq"),
        check_vma=False,
    )
```

```python
import functools
import math

import jax
import jax.numpy as jnp
import numpy as np
from jax import lax
from jax.experimental import pallas as pl
from jax.experimental.pallas import tpu as pltpu
from jax.sharding import PartitionSpec as P

BL = 128
NB = 16
HALF = 0.025


def split(m):
    hi = m.astype(jnp.bfloat16)
    return hi, (m - np.asarray(hi, np.float64)).astype(jnp.bfloat16)


@functools.cache
def tables():
    nodes = 64
    theta = (np.arange(nodes) + 0.5) * np.pi / nodes
    t = np.arange(BL + 1)
    f = np.exp(-HALF * (1 + np.cos(theta))[:, None] * t[None, :])
    psi = np.stack(
        [(2.0 if n else 1.0) / nodes * (np.cos(n * theta) @ f) for n in range(NB)]
    )
    half = BL // 2
    ang = np.pi * np.outer(np.arange(BL), 2 * np.arange(half) + 1) / BL
    c, s = np.cos(ang), np.sin(ang)
    z = np.zeros_like(c)
    fwd = np.block([[c, z, -s, z], [z, c, z, -s]])
    inv = np.block([[c, z, -s, z], [z, c, z, -s]]).T * (2.0 / BL)
    spec = np.concatenate([psi[:, :BL] @ c] * 2 + [-psi[:, :BL] @ s] * 2, axis=1)
    unit = np.concatenate([np.ones((1, BL)), np.zeros((1, BL))], axis=1)
    spec = np.concatenate([spec, unit, np.zeros((15, 2 * BL))], axis=0)
    rev = psi[:, BL - 1 :: -1][:, :BL]
    zr = np.zeros_like(rev)
    mom = np.block([[rev, zr], [zr, rev]])
    nxt = psi[:, 1 : BL + 1]
    car = np.block([[nxt, zr], [zr, nxt]])
    sh, sl = split(spec)
    mh, ml = split(mom)
    ch, cl = split(car)
    sel = np.zeros((8, 6 * 128))
    for i in range(3):
        sel[2 * i + 1, (2 * i) * 128] = 1
        sel[2 * i, (2 * i + 1) * 128] = 1
        sel[2 * i + 1, (2 * i + 1) * 128 + 1] = 1
    wide = np.kron(np.eye(9), np.ones((1, 128)))
    wide = np.concatenate([wide, np.zeros((7, 9 * 128))], axis=0)
    wide = np.concatenate([wide, wide], axis=0)
    cat = lambda *a: np.concatenate(a, axis=0)
    b16 = lambda a: a.astype(jnp.bfloat16)
    return dict(
        fwd=b16(fwd), inv=b16(inv), spec=cat(sh, sh, sl), mom=cat(mh, ml),
        car=cat(ch, ch, cl), sel=b16(sel), wide=b16(wide),
    )


def rowdot(a, b):
    return lax.dot_general(a, b, (((0,), (0,)), ((), ())), preferred_element_type=jnp.float32)


def three(m):
    hi = m.astype(jnp.bfloat16)
    lo = (m - hi.astype(jnp.float32)).astype(jnp.bfloat16)
    return jnp.concatenate([hi, lo, hi], axis=0)


def dot(a, b):
    return jnp.dot(a, b, preferred_element_type=jnp.float32)


def two(m):
    hi = m.astype(jnp.bfloat16)
    lo = (m - hi.astype(jnp.float32)).astype(jnp.bfloat16)
    return jnp.concatenate([hi, lo], axis=0)


def series(decay, cheb_ref):
    xi = decay * (1.0 / HALF) - 1.0
    a, b = jnp.ones_like(xi), xi
    for n in range(NB):
        cheb_ref[n * 16 : n * 16 + 16] = a
        a, b = b, 2.0 * xi * b - a


def feat(x, w_ref, rows, h1, h2, first):
    lane = lax.broadcasted_iota(jnp.int32, (x.shape[0], 128), 1)
    w0, w1, w2 = (w_ref[rows, (first + i) * 128 : (first + i + 1) * 128] for i in range(3))
    out = []
    for i in range(x.shape[1] // 128):
        c = x[:, i * 128 : (i + 1) * 128].astype(jnp.float32)
        r1, r2 = pltpu.roll(c, 1, 1), pltpu.roll(c, 2, 1)
        out.append(w0 * c + w1 * jnp.where(lane < 1, h1, r1) + w2 * jnp.where(lane < 2, h2, r2))
        h1, h2 = r1, r2
    return out


ROWS = 64


def front(p_ref, halo_ref, w_ref, decay_ref, sel_ref, wide_ref, mom_ref,
          mixed_ref, ends_ref, last_ref, power_ref,
          hr_ref, wide_w, cheb_ref):
    tile, length = p_ref.shape[1:]
    hr_ref[...] = rowdot(halo_ref[...], sel_ref[:, 256:])
    wide_w[...] = rowdot(two(w_ref[...]), wide_ref[:, 384:])
    series(decay_ref[...], cheb_ref)

    @pl.loop(0, tile // ROWS)
    def _(r):
        rows = pl.ds(pl.multiple_of(r * ROWS, ROWS), ROWS)
        k = feat(p_ref[0, rows, :], wide_w, rows, hr_ref[rows, 0:128], hr_ref[rows, 128:256], 0)
        v = feat(p_ref[1, rows, :], wide_w, rows, hr_ref[rows, 256:384], hr_ref[rows, 384:512], 3)
        for i in range(len(k)):
            mixed_ref[rows, i * 128 : (i + 1) * 128] = (k[i] * v[i]).astype(jnp.bfloat16)

    step = jnp.exp(-BL * decay_ref[...])
    total = None
    for pair in range(length // 256):
        m = lax.dot_general(
            mom_ref[...], mixed_ref[:, pair * 256 : (pair + 1) * 256],
            (((1,), (1,)), ((), ())), preferred_element_type=jnp.float32)
        m = m[:32] + m[32:]
        for b in range(2):
            e = cheb_ref[0:16] * m[b * 16 : b * 16 + 1]
            for i in range(1, NB):
                e = e + cheb_ref[i * 16 : i * 16 + 16] * m[b * 16 + i : b * 16 + i + 1]
            ends_ref[(pair * 2 + b) * 16 : (pair * 2 + b + 1) * 16] = e
            total = e if total is None else step * total + e
    last_ref[...] = total.astype(last_ref.dtype)
    power_ref[...] = jnp.exp(-length * decay_ref[...])


def exchange(n, last_ref, power_ref, init_ref, inbox, send_sem, recv_sem):
    me = lax.axis_index("seq")
    barrier = pltpu.get_barrier_semaphore()

    @pl.loop(0, n)
    def _(j):
        @pl.when(j != me)
        def _():
            pl.semaphore_signal(barrier, inc=1, device_id={"seq": j}, device_id_type=pl.DeviceIdType.MESH)

    pl.semaphore_wait(barrier, n - 1)

    def copy(j, source):
        return pltpu.make_async_remote_copy(
            src_ref=last_ref, dst_ref=inbox.at[source],
            send_sem=send_sem.at[j], recv_sem=recv_sem.at[source],
            device_id={"seq": j}, device_id_type=pl.DeviceIdType.MESH)

    @pl.loop(0, n)
    def _(j):
        @pl.when(j > me)
        def _():
            copy(j, me).start()

    init_ref[...] = jnp.zeros_like(init_ref)

    @pl.loop(0, n)
    def _(j):
        @pl.when(j < me)
        def _():
            copy(me, j).wait_recv()
            init_ref[...] = power_ref[...] * init_ref[...] + inbox[j].astype(jnp.float32)

    @pl.loop(0, n)
    def _(j):
        @pl.when(j > me)
        def _():
            copy(j, me).wait_send()


def back(q_ref, mixed_ref, halo_ref, w_ref, decay_ref, residue_ref, skip_ref, ends_ref, init_ref,
         sel_ref, wide_ref, fwd_ref, inv_ref, spec_ref, car_ref,
         out_ref, hr_ref, h_ref, y_ref, wide_w, cheb_ref):
    tile = mixed_ref.shape[0]
    hr_ref[...] = rowdot(halo_ref[...], sel_ref[:, :256])
    wide_w[...] = rowdot(two(w_ref[...]), wide_ref[:, :384])
    series(decay_ref[...], cheb_ref)
    step = jnp.exp(-BL * decay_ref[...])
    fold = 1.0 / (1.0 + step)
    weight = residue_ref[...] * jnp.sqrt(2.0 * decay_ref[...])
    wv = weight * fold
    g = [jnp.sum(wv * cheb_ref[n * 16 : n * 16 + 16], axis=0, keepdims=True) for n in range(NB)]
    g = jnp.concatenate(g + [skip_ref[...], jnp.zeros((15, tile), jnp.float32)], axis=0)
    h_ref[...] = rowdot(three(g), spec_ref[...])
    state = init_ref[...]
    for pair in range(mixed_ref.shape[1] // 256):
        c = []
        for b in range(2):
            e = ends_ref[(pair * 2 + b) * 16 : (pair * 2 + b + 1) * 16]
            p = weight * (state + fold * e)
            state = step * state + e
            c += [jnp.sum(p * cheb_ref[n * 16 : n * 16 + 16], axis=0, keepdims=True) for n in range(NB)]
        cols = slice(pair * 256, pair * 256 + 256)
        carried = rowdot(three(jnp.concatenate(c, axis=0)), car_ref[...])
        x = dot(mixed_ref[:, cols], fwd_ref[...])
        xr, xi = x[:, :128], x[:, 128:]
        hr, hi = h_ref[:, :128], h_ref[:, 128:]
        y = jnp.concatenate([xr * hr - xi * hi, xr * hi + xi * hr], axis=1).astype(jnp.bfloat16)
        y_ref[:, cols] = (carried + dot(y, inv_ref[...])).astype(jnp.bfloat16)

    @pl.loop(0, tile // ROWS)
    def _(r):
        rows = pl.ds(pl.multiple_of(r * ROWS, ROWS), ROWS)
        q = feat(q_ref[0, rows, :], wide_w, rows, hr_ref[rows, 0:128], hr_ref[rows, 128:256], 0)
        for i in range(len(q)):
            cols = slice(i * 128, i * 128 + 128)
            out_ref[rows, cols] = (q[i] * y_ref[rows, cols].astype(jnp.float32)).astype(jnp.bfloat16)


def shards(projected, short_weight, skip_weight, decay_rates, residues):
    channels, length = projected.shape[1:]
    n = lax.axis_size("seq")
    tab = {k: jnp.asarray(v) for k, v in tables().items()}
    tile = math.gcd(512, channels)
    blocks = length // BL
    tail = jnp.swapaxes(projected[:, :, length - 2 :], 1, 2)
    halo = lax.ppermute(tail, "seq", [(i, i + 1) for i in range(n - 1)])
    halo = jnp.pad(halo.reshape(6, channels), ((0, 2), (0, 0)))
    taps = jnp.swapaxes(short_weight, 1, 2).reshape(9, channels)
    taps = jnp.pad(taps, ((0, 7), (0, 0)))
    decay, residue = decay_rates.T, residues.T

    full = lambda a: pl.BlockSpec(a.shape, lambda i: (0,) * a.ndim)
    lanes = lambda r: pl.BlockSpec((r, tile), lambda i: (0, i))
    rows = pl.BlockSpec((tile, length), lambda i: (i, 0))
    limit = 56 * 2**20
    count = channels // tile
    names = ("sel", "wide", "mom")
    mixed, ends, last, power = pl.pallas_call(
        front,
        grid=(count,),
        in_specs=[pl.BlockSpec((pl.Element(2), pl.Element(tile), pl.Element(length)), lambda i: (1, i * tile, 0)),
                  lanes(8), lanes(16), lanes(16)] + [full(tab[k]) for k in names],
        out_specs=[rows, lanes(blocks * 16), lanes(16), lanes(16)],
        out_shape=[
            jax.ShapeDtypeStruct((channels, length), jnp.bfloat16),
            jax.ShapeDtypeStruct((blocks * 16, channels), jnp.float32),
            jax.ShapeDtypeStruct((16, channels), jnp.bfloat16),
            jax.ShapeDtypeStruct((16, channels), jnp.float32),
        ],
        scratch_shapes=[
            pltpu.VMEM((tile, 512), jnp.float32),
            pltpu.VMEM((tile, 6 * 128), jnp.float32),
            pltpu.VMEM((NB * 16, tile), jnp.float32),
        ],
        compiler_params=pltpu.CompilerParams(vmem_limit_bytes=limit),
        name="front",
    )(projected, halo, taps, decay, *[tab[k] for k in names])
    init = pl.pallas_call(
        functools.partial(exchange, n),
        in_specs=[pl.BlockSpec(memory_space=pltpu.VMEM)] * 2,
        out_specs=pl.BlockSpec(memory_space=pltpu.VMEM),
        out_shape=jax.ShapeDtypeStruct((16, channels), jnp.float32),
        scratch_shapes=[
            pltpu.VMEM((n, 16, channels), jnp.bfloat16),
            pltpu.SemaphoreType.DMA((n,)),
            pltpu.SemaphoreType.DMA((n,)),
        ],
        compiler_params=pltpu.CompilerParams(collective_id=0, has_side_effects=True),
        name="exchange",
    )(last, power)
    names = ("sel", "wide", "fwd", "inv", "spec", "car")
    return pl.pallas_call(
        back,
        grid=(count,),
        in_specs=[pl.BlockSpec((1, tile, length), lambda i: (0, i, 0)), rows, lanes(8), lanes(16), lanes(16),
                  lanes(16), lanes(1), lanes(blocks * 16), lanes(16)] + [full(tab[k]) for k in names],
        out_specs=rows,
        out_shape=jax.ShapeDtypeStruct((channels, length), jnp.bfloat16),
        scratch_shapes=[
            pltpu.VMEM((tile, 256), jnp.float32),
            pltpu.VMEM((tile, 256), jnp.float32),
            pltpu.VMEM((tile, length), jnp.bfloat16),
            pltpu.VMEM((tile, 3 * 128), jnp.float32),
            pltpu.VMEM((NB * 16, tile), jnp.float32),
        ],
        compiler_params=pltpu.CompilerParams(vmem_limit_bytes=limit),
        name="back",
    )(projected, mixed, halo, taps, decay, residue, skip_weight[None], ends, init, *[tab[k] for k in names])


def solution(mesh):
    return jax.shard_map(
        shards,
        mesh=mesh,
        in_specs=(
            P(None, "fsdp", "seq"),
            P(None, "fsdp", None),
            P("fsdp"),
            P("fsdp", None),
            P("fsdp", None),
        ),
        out_specs=P("fsdp", "seq"),
        check_vma=False,
    )
```

```python
import functools
import math

import jax
import jax.numpy as jnp
import numpy as np
from jax import lax
from jax.experimental import pallas as pl
from jax.experimental.pallas import tpu as pltpu
from jax.sharding import PartitionSpec as P

BL = 128
NB = 16
HALF = 0.025


def split(m):
    hi = m.astype(jnp.bfloat16)
    return hi, (m - np.asarray(hi, np.float64)).astype(jnp.bfloat16)


@functools.cache
def tables():
    nodes = 64
    theta = (np.arange(nodes) + 0.5) * np.pi / nodes
    t = np.arange(BL + 1)
    f = np.exp(-HALF * (1 + np.cos(theta))[:, None] * t[None, :])
    psi = np.stack(
        [(2.0 if n else 1.0) / nodes * (np.cos(n * theta) @ f) for n in range(NB)]
    )
    half = BL // 2
    ang = np.pi * np.outer(np.arange(BL), 2 * np.arange(half) + 1) / BL
    c, s = np.cos(ang), np.sin(ang)
    z = np.zeros_like(c)
    fwd = np.block([[c, z, -s, z], [z, c, z, -s]])
    inv = np.block([[c, z, -s, z], [z, c, z, -s]]).T * (2.0 / BL)
    spec = np.concatenate([psi[:, :BL] @ c] * 2 + [-psi[:, :BL] @ s] * 2, axis=1)
    unit = np.concatenate([np.ones((1, BL)), np.zeros((1, BL))], axis=1)
    spec = np.concatenate([spec, unit, np.zeros((15, 2 * BL))], axis=0)
    rev = psi[:, BL - 1 :: -1][:, :BL]
    zr = np.zeros_like(rev)
    mom = np.block([[rev, zr], [zr, rev]])
    nxt = psi[:, 1 : BL + 1]
    car = np.block([[nxt, zr], [zr, nxt]])
    sh, sl = split(spec)
    mh, ml = split(mom)
    ch, cl = split(car)
    sel = np.zeros((8, 6 * 128))
    for i in range(3):
        sel[2 * i + 1, (2 * i) * 128] = 1
        sel[2 * i, (2 * i + 1) * 128] = 1
        sel[2 * i + 1, (2 * i + 1) * 128 + 1] = 1
    wide = np.kron(np.eye(9), np.ones((1, 128)))
    wide = np.concatenate([wide, np.zeros((7, 9 * 128))], axis=0)
    wide = np.concatenate([wide, wide], axis=0)
    cat = lambda *a: np.concatenate(a, axis=0)
    b16 = lambda a: a.astype(jnp.bfloat16)
    return dict(
        fwd=b16(fwd), inv=b16(inv), spec=cat(sh, sh, sl), mom=cat(mh, ml),
        car=cat(ch, ch, cl), sel=b16(sel), wide=b16(wide),
    )


def rowdot(a, b):
    return lax.dot_general(a, b, (((0,), (0,)), ((), ())), preferred_element_type=jnp.float32)


def three(m):
    hi = m.astype(jnp.bfloat16)
    lo = (m - hi.astype(jnp.float32)).astype(jnp.bfloat16)
    return jnp.concatenate([hi, lo, hi], axis=0)


def dot(a, b):
    return jnp.dot(a, b, preferred_element_type=jnp.float32)


def two(m):
    hi = m.astype(jnp.bfloat16)
    lo = (m - hi.astype(jnp.float32)).astype(jnp.bfloat16)
    return jnp.concatenate([hi, lo], axis=0)


def padded(m, count):
    m = m.astype(jnp.float32)
    return jnp.concatenate([m, jnp.zeros((count - m.shape[0], m.shape[1]), jnp.float32)], axis=0)


def series(decay, cheb_ref):
    xi = decay * (1.0 / HALF) - 1.0
    a, b = jnp.ones_like(xi), xi
    for n in range(NB):
        cheb_ref[n * 16 : n * 16 + 16] = a
        a, b = b, 2.0 * xi * b - a


def feat(x, w_ref, rows, h1, h2, first):
    lane = lax.broadcasted_iota(jnp.int32, (x.shape[0], 128), 1)
    w0, w1, w2 = (w_ref[rows, (first + i) * 128 : (first + i + 1) * 128] for i in range(3))
    out = []
    for i in range(x.shape[1] // 128):
        c = x[:, i * 128 : (i + 1) * 128].astype(jnp.float32)
        r1, r2 = pltpu.roll(c, 1, 1), pltpu.roll(c, 2, 1)
        out.append(w0 * c + w1 * jnp.where(lane < 1, h1, r1) + w2 * jnp.where(lane < 2, h2, r2))
        h1, h2 = r1, r2
    return out


ROWS = 64


def front(p_ref, halo_ref, w_ref, decay_ref, sel_ref, wide_ref, mom_ref,
          mixed_ref, ends_ref, last_ref, power_ref,
          hr_ref, wide_w, cheb_ref):
    tile, length = p_ref.shape[1:]
    hr_ref[...] = rowdot(padded(halo_ref[...], 8).astype(jnp.bfloat16), sel_ref[:, 256:])
    wide_w[...] = rowdot(two(padded(w_ref[...], 16)), wide_ref[:, 384:])
    series(decay_ref[...], cheb_ref)

    @pl.loop(0, tile // ROWS)
    def _(r):
        rows = pl.ds(pl.multiple_of(r * ROWS, ROWS), ROWS)
        k = feat(p_ref[0, rows, :], wide_w, rows, hr_ref[rows, 0:128], hr_ref[rows, 128:256], 0)
        v = feat(p_ref[1, rows, :], wide_w, rows, hr_ref[rows, 256:384], hr_ref[rows, 384:512], 3)
        for i in range(len(k)):
            mixed_ref[rows, i * 128 : (i + 1) * 128] = (k[i] * v[i]).astype(jnp.bfloat16)

    step = jnp.exp(-BL * decay_ref[...])
    total = None
    for pair in range(length // 256):
        m = lax.dot_general(
            mom_ref[...], mixed_ref[:, pair * 256 : (pair + 1) * 256],
            (((1,), (1,)), ((), ())), preferred_element_type=jnp.float32)
        m = m[:32] + m[32:]
        for b in range(2):
            e = cheb_ref[0:16] * m[b * 16 : b * 16 + 1]
            for i in range(1, NB):
                e = e + cheb_ref[i * 16 : i * 16 + 16] * m[b * 16 + i : b * 16 + i + 1]
            ends_ref[(pair * 2 + b) * 16 : (pair * 2 + b + 1) * 16] = e
            total = e if total is None else step * total + e
    last_ref[...] = total.astype(last_ref.dtype)
    power_ref[...] = jnp.exp(-length * decay_ref[...])


def exchange(n, last_ref, power_ref, init_ref, peer, pair, inbox, give, got, send_sem, recv_sem, swap_send, swap_recv):
    me = lax.axis_index("seq")
    odd = lax.rem(me, 2)
    partner = me + 1 - 2 * odd
    half = last_ref.shape[1] // 2
    own = pl.ds(pl.multiple_of(odd * half, half), half)
    other = pl.ds(pl.multiple_of((1 - odd) * half, half), half)
    barrier = pltpu.get_barrier_semaphore()

    def greet(j):
        pl.semaphore_signal(barrier, inc=1, device_id={"seq": j}, device_id_type=pl.DeviceIdType.MESH)

    greet(partner)

    @pl.loop(0, n // 2)
    def _(i):
        @pl.when(2 * i + odd != me)
        def _():
            greet(2 * i + odd)

    pl.semaphore_wait(barrier, n // 2)

    def swap(src, dst, i):
        return pltpu.make_async_remote_copy(
            src_ref=src, dst_ref=dst, send_sem=swap_send.at[i], recv_sem=swap_recv.at[i],
            device_id={"seq": partner}, device_id_type=pl.DeviceIdType.MESH)

    def copy(i, source):
        return pltpu.make_async_remote_copy(
            src_ref=pair, dst_ref=inbox.at[source], send_sem=send_sem.at[i], recv_sem=recv_sem.at[source],
            device_id={"seq": 2 * i + odd}, device_id_type=pl.DeviceIdType.MESH)

    at = lax.div(me, 2)
    first = swap(last_ref.at[:, other], peer, 0)
    first.start()
    power = power_ref[:, own]
    mine = last_ref[:, own].astype(jnp.float32)
    first.wait_recv()
    theirs = peer[...].astype(jnp.float32)
    even = odd == 0
    e0 = jnp.where(even, mine, theirs)
    e1 = jnp.where(even, theirs, mine)
    pair[...] = (power * e0 + e1).astype(pair.dtype)

    @pl.loop(0, n // 2)
    def _(i):
        @pl.when(i > at)
        def _():
            copy(i, at).start()

    init_ref[:, own] = jnp.zeros((16, half), jnp.float32)

    @pl.loop(0, n // 2)
    def _(i):
        @pl.when(i < at)
        def _():
            copy(at, i).wait_recv()
            init_ref[:, own] = power * power * init_ref[:, own] + inbox[i].astype(jnp.float32)

    start = init_ref[:, own]
    later = power * start + e0
    give[...] = jnp.where(even, later, start).astype(give.dtype)
    second = swap(give, got, 1)
    second.start()
    init_ref[:, own] = jnp.where(even, start, later)
    second.wait_recv()
    init_ref[:, other] = got[...].astype(jnp.float32)
    first.wait_send()
    second.wait_send()

    @pl.loop(0, n // 2)
    def _(i):
        @pl.when(i > at)
        def _():
            copy(i, at).wait_send()


def back(q_ref, mixed_ref, halo_ref, w_ref, decay_ref, residue_ref, skip_ref, ends_ref, init_ref,
         sel_ref, wide_ref, fwd_ref, inv_ref, spec_ref, car_ref,
         out_ref, hr_ref, h_ref, y_ref, wide_w, cheb_ref):
    tile = mixed_ref.shape[0]
    hr_ref[...] = rowdot(padded(halo_ref[...], 8).astype(jnp.bfloat16), sel_ref[:, :256])
    wide_w[...] = rowdot(two(padded(w_ref[...], 16)), wide_ref[:, :384])
    series(decay_ref[...], cheb_ref)
    step = jnp.exp(-BL * decay_ref[...])
    fold = 1.0 / (1.0 + step)
    weight = residue_ref[...] * jnp.sqrt(2.0 * decay_ref[...])
    wv = weight * fold
    g = [jnp.sum(wv * cheb_ref[n * 16 : n * 16 + 16], axis=0, keepdims=True) for n in range(NB)]
    g = jnp.concatenate(g + [skip_ref[...], jnp.zeros((15, tile), jnp.float32)], axis=0)
    h_ref[...] = rowdot(three(g), spec_ref[...])
    state = init_ref[...]
    for pair in range(mixed_ref.shape[1] // 256):
        c = []
        for b in range(2):
            e = ends_ref[(pair * 2 + b) * 16 : (pair * 2 + b + 1) * 16]
            p = weight * (state + fold * e)
            state = step * state + e
            c += [jnp.sum(p * cheb_ref[n * 16 : n * 16 + 16], axis=0, keepdims=True) for n in range(NB)]
        cols = slice(pair * 256, pair * 256 + 256)
        carried = rowdot(three(jnp.concatenate(c, axis=0)), car_ref[...])
        x = dot(mixed_ref[:, cols], fwd_ref[...])
        xr, xi = x[:, :128], x[:, 128:]
        hr, hi = h_ref[:, :128], h_ref[:, 128:]
        y = jnp.concatenate([xr * hr - xi * hi, xr * hi + xi * hr], axis=1).astype(jnp.bfloat16)
        y_ref[:, cols] = (carried + dot(y, inv_ref[...])).astype(jnp.bfloat16)

    @pl.loop(0, tile // ROWS)
    def _(r):
        rows = pl.ds(pl.multiple_of(r * ROWS, ROWS), ROWS)
        q = feat(q_ref[0, rows, :], wide_w, rows, hr_ref[rows, 0:128], hr_ref[rows, 128:256], 0)
        for i in range(len(q)):
            cols = slice(i * 128, i * 128 + 128)
            out_ref[rows, cols] = (q[i] * y_ref[rows, cols].astype(jnp.float32)).astype(jnp.bfloat16)


def shards(projected, short_weight, skip_weight, decay_rates, residues):
    channels, length = projected.shape[1:]
    n = lax.axis_size("seq")
    tab = {k: jnp.asarray(v) for k, v in tables().items()}
    tile = math.gcd(512, channels)
    blocks = length // BL
    tail = jnp.swapaxes(projected[:, :, length - 2 :], 1, 2)
    halo = lax.ppermute(tail, "seq", [(i, i + 1) for i in range(n - 1)])
    halo = halo.reshape(6, channels)
    taps = jnp.swapaxes(short_weight, 1, 2).reshape(9, channels)
    decay, residue = decay_rates.T, residues.T

    full = lambda a: pl.BlockSpec(a.shape, lambda i: (0,) * a.ndim)
    lanes = lambda r: pl.BlockSpec((r, tile), lambda i: (0, i))
    rows = pl.BlockSpec((tile, length), lambda i: (i, 0))
    limit = 56 * 2**20
    count = channels // tile
    names = ("sel", "wide", "mom")
    mixed, ends, last, power = pl.pallas_call(
        front,
        grid=(count,),
        in_specs=[pl.BlockSpec((pl.Element(2), pl.Element(tile), pl.Element(length)), lambda i: (1, i * tile, 0)),
                  lanes(6), lanes(9), lanes(16)] + [full(tab[k]) for k in names],
        out_specs=[rows, lanes(blocks * 16), lanes(16), lanes(16)],
        out_shape=[
            jax.ShapeDtypeStruct((channels, length), jnp.bfloat16),
            jax.ShapeDtypeStruct((blocks * 16, channels), jnp.float32),
            jax.ShapeDtypeStruct((16, channels), jnp.bfloat16),
            jax.ShapeDtypeStruct((16, channels), jnp.float32),
        ],
        scratch_shapes=[
            pltpu.VMEM((tile, 512), jnp.float32),
            pltpu.VMEM((tile, 6 * 128), jnp.float32),
            pltpu.VMEM((NB * 16, tile), jnp.float32),
        ],
        compiler_params=pltpu.CompilerParams(vmem_limit_bytes=limit),
        name="front",
    )(projected, halo, taps, decay, *[tab[k] for k in names])
    init = pl.pallas_call(
        functools.partial(exchange, n),
        in_specs=[pl.BlockSpec(memory_space=pltpu.VMEM)] * 2,
        out_specs=pl.BlockSpec(memory_space=pltpu.VMEM),
        out_shape=jax.ShapeDtypeStruct((16, channels), jnp.float32),
        scratch_shapes=[
            pltpu.VMEM((16, channels // 2), jnp.bfloat16),
            pltpu.VMEM((16, channels // 2), jnp.bfloat16),
            pltpu.VMEM((n // 2, 16, channels // 2), jnp.bfloat16),
            pltpu.VMEM((16, channels // 2), jnp.bfloat16),
            pltpu.VMEM((16, channels // 2), jnp.bfloat16),
            pltpu.SemaphoreType.DMA((n // 2,)),
            pltpu.SemaphoreType.DMA((n // 2,)),
            pltpu.SemaphoreType.DMA((2,)),
            pltpu.SemaphoreType.DMA((2,)),
        ],
        compiler_params=pltpu.CompilerParams(collective_id=0, has_side_effects=True),
        name="exchange",
    )(last, power)
    names = ("sel", "wide", "fwd", "inv", "spec", "car")
    return pl.pallas_call(
        back,
        grid=(count,),
        in_specs=[pl.BlockSpec((1, tile, length), lambda i: (0, i, 0)), rows, lanes(6), lanes(9), lanes(16),
                  lanes(16), lanes(1), lanes(blocks * 16), lanes(16)] + [full(tab[k]) for k in names],
        out_specs=rows,
        out_shape=jax.ShapeDtypeStruct((channels, length), jnp.bfloat16),
        scratch_shapes=[
            pltpu.VMEM((tile, 256), jnp.float32),
            pltpu.VMEM((tile, 256), jnp.float32),
            pltpu.VMEM((tile, length), jnp.bfloat16),
            pltpu.VMEM((tile, 3 * 128), jnp.float32),
            pltpu.VMEM((NB * 16, tile), jnp.float32),
        ],
        compiler_params=pltpu.CompilerParams(vmem_limit_bytes=limit),
        name="back",
    )(projected, mixed, halo, taps, decay, residue, skip_weight[None], ends, init, *[tab[k] for k in names])


def solution(mesh):
    return jax.shard_map(
        shards,
        mesh=mesh,
        in_specs=(
            P(None, "fsdp", "seq"),
            P(None, "fsdp", None),
            P("fsdp"),
            P("fsdp", None),
            P("fsdp", None),
        ),
        out_specs=P("fsdp", "seq"),
        check_vma=False,
    )
```

```python
import functools
import math

import jax
import jax.numpy as jnp
import numpy as np
from jax import lax
from jax.experimental import pallas as pl
from jax.experimental.pallas import tpu as pltpu
from jax.sharding import PartitionSpec as P

BL = 128
NB = 16
HALF = 0.025


def split(m):
    hi = m.astype(jnp.bfloat16)
    return hi, (m - np.asarray(hi, np.float64)).astype(jnp.bfloat16)


@functools.cache
def tables():
    nodes = 64
    theta = (np.arange(nodes) + 0.5) * np.pi / nodes
    t = np.arange(BL + 1)
    f = np.exp(-HALF * (1 + np.cos(theta))[:, None] * t[None, :])
    psi = np.stack(
        [(2.0 if n else 1.0) / nodes * (np.cos(n * theta) @ f) for n in range(NB)]
    )
    half = BL // 2
    ang = np.pi * np.outer(np.arange(BL), 2 * np.arange(half) + 1) / BL
    c, s = np.cos(ang), np.sin(ang)
    z = np.zeros_like(c)
    fwd = np.block([[c, z, -s, z], [z, c, z, -s]])
    inv = np.block([[c, z, -s, z], [z, c, z, -s]]).T * (2.0 / BL)
    spec = np.concatenate([psi[:, :BL] @ c] * 2 + [-psi[:, :BL] @ s] * 2, axis=1)
    unit = np.concatenate([np.ones((1, BL)), np.zeros((1, BL))], axis=1)
    spec = np.concatenate([spec, unit, np.zeros((15, 2 * BL))], axis=0)
    rev = psi[:, BL - 1 :: -1][:, :BL]
    zr = np.zeros_like(rev)
    mom = np.block([[rev, zr], [zr, rev]])
    nxt = psi[:, 1 : BL + 1]
    car = np.block([[nxt, zr], [zr, nxt]])
    sh, sl = split(spec)
    mh, ml = split(mom)
    ch, cl = split(car)
    sel = np.zeros((8, 6 * 128))
    for i in range(3):
        sel[2 * i + 1, (2 * i) * 128] = 1
        sel[2 * i, (2 * i + 1) * 128] = 1
        sel[2 * i + 1, (2 * i + 1) * 128 + 1] = 1
    pick = np.zeros((3, 8, 128))
    for i in range(3):
        pick[i, 2 * i, 126] = pick[i, 2 * i + 1, 127] = 1
    wide = np.kron(np.eye(9), np.ones((1, 128)))
    wide = np.concatenate([wide, np.zeros((7, 9 * 128))], axis=0)
    wide = np.concatenate([wide, wide], axis=0)
    cat = lambda *a: np.concatenate(a, axis=0)
    b16 = lambda a: a.astype(jnp.bfloat16)
    return dict(
        fwd=b16(fwd), inv=b16(inv), spec=cat(sh, sh, sl), mom=cat(mh, ml),
        car=cat(ch, ch, cl), sel=b16(sel), pick=b16(pick), wide=b16(wide),
    )


def rowdot(a, b):
    return lax.dot_general(a, b, (((0,), (0,)), ((), ())), preferred_element_type=jnp.float32)


def three(m):
    hi = m.astype(jnp.bfloat16)
    lo = (m - hi.astype(jnp.float32)).astype(jnp.bfloat16)
    return jnp.concatenate([hi, lo, hi], axis=0)


def dot(a, b):
    return jnp.dot(a, b, preferred_element_type=jnp.float32)


def two(m):
    hi = m.astype(jnp.bfloat16)
    lo = (m - hi.astype(jnp.float32)).astype(jnp.bfloat16)
    return jnp.concatenate([hi, lo], axis=0)


def padded(ref, count):
    parts = [ref[i] for i in range(3)]
    return jnp.concatenate(parts + [jnp.zeros((count - 9, ref.shape[2]), jnp.float32)], axis=0)


def last_two(p_ref, pick_ref, out_ref):
    picked = [
        lax.dot_general(pick_ref[i], p_ref[i], (((1,), (1,)), ((), ())), preferred_element_type=jnp.float32)
        for i in range(3)
    ]
    out_ref[...] = (picked[0] + picked[1] + picked[2]).astype(out_ref.dtype)


def series(decay, cheb_ref):
    xi = decay * (1.0 / HALF) - 1.0
    a, b = jnp.ones_like(xi), xi
    for n in range(NB):
        cheb_ref[n * 16 : n * 16 + 16] = a
        a, b = b, 2.0 * xi * b - a


def feat(x, w_ref, rows, h1, h2, first):
    lane = lax.broadcasted_iota(jnp.int32, (x.shape[0], 128), 1)
    w0, w1, w2 = (w_ref[rows, (first + i) * 128 : (first + i + 1) * 128] for i in range(3))
    out = []
    for i in range(x.shape[1] // 128):
        c = x[:, i * 128 : (i + 1) * 128].astype(jnp.float32)
        r1, r2 = pltpu.roll(c, 1, 1), pltpu.roll(c, 2, 1)
        out.append(w0 * c + w1 * jnp.where(lane < 1, h1, r1) + w2 * jnp.where(lane < 2, h2, r2))
        h1, h2 = r1, r2
    return out


ROWS = 64


def front(p_ref, halo_ref, w_ref, decay_ref, sel_ref, wide_ref, mom_ref,
          mixed_ref, ends_ref, last_ref, power_ref,
          hr_ref, wide_w, cheb_ref):
    tile, length = p_ref.shape[1:]
    hr_ref[...] = rowdot(halo_ref[...], sel_ref[:, 256:])
    wide_w[...] = rowdot(two(padded(w_ref, 16)), wide_ref[:, 384:])
    series(decay_ref[...], cheb_ref)

    @pl.loop(0, tile // ROWS)
    def _(r):
        rows = pl.ds(pl.multiple_of(r * ROWS, ROWS), ROWS)
        k = feat(p_ref[0, rows, :], wide_w, rows, hr_ref[rows, 0:128], hr_ref[rows, 128:256], 0)
        v = feat(p_ref[1, rows, :], wide_w, rows, hr_ref[rows, 256:384], hr_ref[rows, 384:512], 3)
        for i in range(len(k)):
            mixed_ref[rows, i * 128 : (i + 1) * 128] = (k[i] * v[i]).astype(jnp.bfloat16)

    step = jnp.exp(-BL * decay_ref[...])
    total = None
    for pair in range(length // 256):
        m = lax.dot_general(
            mom_ref[...], mixed_ref[:, pair * 256 : (pair + 1) * 256],
            (((1,), (1,)), ((), ())), preferred_element_type=jnp.float32)
        m = m[:32] + m[32:]
        for b in range(2):
            e = cheb_ref[0:16] * m[b * 16 : b * 16 + 1]
            for i in range(1, NB):
                e = e + cheb_ref[i * 16 : i * 16 + 16] * m[b * 16 + i : b * 16 + i + 1]
            ends_ref[(pair * 2 + b) * 16 : (pair * 2 + b + 1) * 16] = e
            total = e if total is None else step * total + e
    last_ref[...] = total.astype(last_ref.dtype)
    power_ref[...] = jnp.exp(-length * decay_ref[...])


def exchange(n, last_ref, power_ref, init_ref, peer, pair, inbox, give, got, send_sem, recv_sem, swap_send, swap_recv):
    me = lax.axis_index("seq")
    odd = lax.rem(me, 2)
    partner = me + 1 - 2 * odd
    half = last_ref.shape[1] // 2
    own = pl.ds(pl.multiple_of(odd * half, half), half)
    other = pl.ds(pl.multiple_of((1 - odd) * half, half), half)
    barrier = pltpu.get_barrier_semaphore()

    def greet(j):
        pl.semaphore_signal(barrier, inc=1, device_id={"seq": j}, device_id_type=pl.DeviceIdType.MESH)

    greet(partner)

    @pl.loop(0, n // 2)
    def _(i):
        @pl.when(2 * i + odd != me)
        def _():
            greet(2 * i + odd)

    pl.semaphore_wait(barrier, n // 2)

    def swap(src, dst, i):
        return pltpu.make_async_remote_copy(
            src_ref=src, dst_ref=dst, send_sem=swap_send.at[i], recv_sem=swap_recv.at[i],
            device_id={"seq": partner}, device_id_type=pl.DeviceIdType.MESH)

    def copy(i, source):
        return pltpu.make_async_remote_copy(
            src_ref=pair, dst_ref=inbox.at[source], send_sem=send_sem.at[i], recv_sem=recv_sem.at[source],
            device_id={"seq": 2 * i + odd}, device_id_type=pl.DeviceIdType.MESH)

    at = lax.div(me, 2)
    first = swap(last_ref.at[:, other], peer, 0)
    first.start()
    power = power_ref[:, own]
    mine = last_ref[:, own].astype(jnp.float32)
    first.wait_recv()
    theirs = peer[...].astype(jnp.float32)
    even = odd == 0
    e0 = jnp.where(even, mine, theirs)
    e1 = jnp.where(even, theirs, mine)
    pair[...] = (power * e0 + e1).astype(pair.dtype)

    @pl.loop(0, n // 2)
    def _(i):
        @pl.when(i > at)
        def _():
            copy(i, at).start()

    init_ref[:, own] = jnp.zeros((16, half), jnp.float32)

    @pl.loop(0, n // 2)
    def _(i):
        @pl.when(i < at)
        def _():
            copy(at, i).wait_recv()
            init_ref[:, own] = power * power * init_ref[:, own] + inbox[i].astype(jnp.float32)

    start = init_ref[:, own]
    later = power * start + e0
    give[...] = jnp.where(even, later, start).astype(give.dtype)
    second = swap(give, got, 1)
    second.start()
    init_ref[:, own] = jnp.where(even, start, later)
    second.wait_recv()
    init_ref[:, other] = got[...].astype(jnp.float32)
    first.wait_send()
    second.wait_send()

    @pl.loop(0, n // 2)
    def _(i):
        @pl.when(i > at)
        def _():
            copy(i, at).wait_send()


def back(q_ref, mixed_ref, halo_ref, w_ref, decay_ref, residue_ref, skip_ref, ends_ref, init_ref,
         sel_ref, wide_ref, fwd_ref, inv_ref, spec_ref, car_ref,
         out_ref, hr_ref, h_ref, y_ref, wide_w, cheb_ref):
    tile = mixed_ref.shape[0]
    hr_ref[...] = rowdot(halo_ref[...], sel_ref[:, :256])
    wide_w[...] = rowdot(two(padded(w_ref, 16)), wide_ref[:, :384])
    series(decay_ref[...], cheb_ref)
    step = jnp.exp(-BL * decay_ref[...])
    fold = 1.0 / (1.0 + step)
    weight = residue_ref[...] * jnp.sqrt(2.0 * decay_ref[...])
    wv = weight * fold
    g = [jnp.sum(wv * cheb_ref[n * 16 : n * 16 + 16], axis=0, keepdims=True) for n in range(NB)]
    g = jnp.concatenate(g + [skip_ref[...], jnp.zeros((15, tile), jnp.float32)], axis=0)
    h_ref[...] = rowdot(three(g), spec_ref[...])
    state = init_ref[...]
    for pair in range(mixed_ref.shape[1] // 256):
        c = []
        for b in range(2):
            e = ends_ref[(pair * 2 + b) * 16 : (pair * 2 + b + 1) * 16]
            p = weight * (state + fold * e)
            state = step * state + e
            c += [jnp.sum(p * cheb_ref[n * 16 : n * 16 + 16], axis=0, keepdims=True) for n in range(NB)]
        cols = slice(pair * 256, pair * 256 + 256)
        carried = rowdot(three(jnp.concatenate(c, axis=0)), car_ref[...])
        x = dot(mixed_ref[:, cols], fwd_ref[...])
        xr, xi = x[:, :128], x[:, 128:]
        hr, hi = h_ref[:, :128], h_ref[:, 128:]
        y = jnp.concatenate([xr * hr - xi * hi, xr * hi + xi * hr], axis=1).astype(jnp.bfloat16)
        y_ref[:, cols] = (carried + dot(y, inv_ref[...])).astype(jnp.bfloat16)

    @pl.loop(0, tile // ROWS)
    def _(r):
        rows = pl.ds(pl.multiple_of(r * ROWS, ROWS), ROWS)
        q = feat(q_ref[0, rows, :], wide_w, rows, hr_ref[rows, 0:128], hr_ref[rows, 128:256], 0)
        for i in range(len(q)):
            cols = slice(i * 128, i * 128 + 128)
            out_ref[rows, cols] = (q[i] * y_ref[rows, cols].astype(jnp.float32)).astype(jnp.bfloat16)


def shards(projected, short_weight, skip_weight, decay_rates, residues):
    channels, length = projected.shape[1:]
    n = lax.axis_size("seq")
    tab = {k: jnp.asarray(v) for k, v in tables().items()}
    tile = math.gcd(512, channels)
    blocks = length // BL
    taps = jnp.swapaxes(short_weight, 1, 2)
    tail = pl.pallas_call(
        last_two,
        grid=(channels // tile,),
        in_specs=[pl.BlockSpec((3, tile, 128), lambda i: (0, i, length // 128 - 1)),
                  pl.BlockSpec((3, 8, 128), lambda i: (0, 0, 0))],
        out_specs=pl.BlockSpec((8, tile), lambda i: (0, i)),
        out_shape=jax.ShapeDtypeStruct((8, channels), jnp.bfloat16),
        compiler_params=pltpu.CompilerParams(vmem_limit_bytes=56 * 2**20),
        name="last_two",
    )(projected, tab["pick"])
    halo = lax.ppermute(tail, "seq", [(i, i + 1) for i in range(n - 1)])
    decay, residue = decay_rates.T, residues.T

    full = lambda a: pl.BlockSpec(a.shape, lambda i: (0,) * a.ndim)
    lanes = lambda r: pl.BlockSpec((r, tile), lambda i: (0, i))
    rows = pl.BlockSpec((tile, length), lambda i: (i, 0))
    limit = 56 * 2**20
    count = channels // tile
    names = ("sel", "wide", "mom")
    mixed, ends, last, power = pl.pallas_call(
        front,
        grid=(count,),
        in_specs=[pl.BlockSpec((pl.Element(2), pl.Element(tile), pl.Element(length)), lambda i: (1, i * tile, 0)),
                  lanes(8), pl.BlockSpec((3, 3, tile), lambda i: (0, 0, i)), lanes(16)] + [full(tab[k]) for k in names],
        out_specs=[rows, lanes(blocks * 16), lanes(16), lanes(16)],
        out_shape=[
            jax.ShapeDtypeStruct((channels, length), jnp.bfloat16),
            jax.ShapeDtypeStruct((blocks * 16, channels), jnp.float32),
            jax.ShapeDtypeStruct((16, channels), jnp.bfloat16),
            jax.ShapeDtypeStruct((16, channels), jnp.float32),
        ],
        scratch_shapes=[
            pltpu.VMEM((tile, 512), jnp.float32),
            pltpu.VMEM((tile, 6 * 128), jnp.float32),
            pltpu.VMEM((NB * 16, tile), jnp.float32),
        ],
        compiler_params=pltpu.CompilerParams(vmem_limit_bytes=limit),
        name="front",
    )(projected, halo, taps, decay, *[tab[k] for k in names])
    init = pl.pallas_call(
        functools.partial(exchange, n),
        in_specs=[pl.BlockSpec(memory_space=pltpu.VMEM)] * 2,
        out_specs=pl.BlockSpec(memory_space=pltpu.VMEM),
        out_shape=jax.ShapeDtypeStruct((16, channels), jnp.float32),
        scratch_shapes=[
            pltpu.VMEM((16, channels // 2), jnp.bfloat16),
            pltpu.VMEM((16, channels // 2), jnp.bfloat16),
            pltpu.VMEM((n // 2, 16, channels // 2), jnp.bfloat16),
            pltpu.VMEM((16, channels // 2), jnp.bfloat16),
            pltpu.VMEM((16, channels // 2), jnp.bfloat16),
            pltpu.SemaphoreType.DMA((n // 2,)),
            pltpu.SemaphoreType.DMA((n // 2,)),
            pltpu.SemaphoreType.DMA((2,)),
            pltpu.SemaphoreType.DMA((2,)),
        ],
        compiler_params=pltpu.CompilerParams(collective_id=0, has_side_effects=True),
        name="exchange",
    )(last, power)
    names = ("sel", "wide", "fwd", "inv", "spec", "car")
    return pl.pallas_call(
        back,
        grid=(count,),
        in_specs=[pl.BlockSpec((1, tile, length), lambda i: (0, i, 0)), rows, lanes(8), pl.BlockSpec((3, 3, tile), lambda i: (0, 0, i)), lanes(16),
                  lanes(16), lanes(1), lanes(blocks * 16), lanes(16)] + [full(tab[k]) for k in names],
        out_specs=rows,
        out_shape=jax.ShapeDtypeStruct((channels, length), jnp.bfloat16),
        scratch_shapes=[
            pltpu.VMEM((tile, 256), jnp.float32),
            pltpu.VMEM((tile, 256), jnp.float32),
            pltpu.VMEM((tile, length), jnp.bfloat16),
            pltpu.VMEM((tile, 3 * 128), jnp.float32),
            pltpu.VMEM((NB * 16, tile), jnp.float32),
        ],
        compiler_params=pltpu.CompilerParams(vmem_limit_bytes=limit),
        name="back",
    )(projected, mixed, halo, taps, decay, residue, skip_weight[None], ends, init, *[tab[k] for k in names])


def solution(mesh):
    return jax.shard_map(
        shards,
        mesh=mesh,
        in_specs=(
            P(None, "fsdp", "seq"),
            P(None, "fsdp", None),
            P("fsdp"),
            P("fsdp", None),
            P("fsdp", None),
        ),
        out_specs=P("fsdp", "seq"),
        check_vma=False,
    )
```

```python
import functools
import math

import jax
import jax.numpy as jnp
import numpy as np
from jax import lax
from jax.experimental import pallas as pl
from jax.experimental.pallas import tpu as pltpu
from jax.sharding import PartitionSpec as P

BL = 128
NB = 16
HALF = 0.025


def split(m):
    hi = m.astype(jnp.bfloat16)
    return hi, (m - np.asarray(hi, np.float64)).astype(jnp.bfloat16)


@functools.cache
def tables():
    nodes = 64
    theta = (np.arange(nodes) + 0.5) * np.pi / nodes
    t = np.arange(BL + 1)
    f = np.exp(-HALF * (1 + np.cos(theta))[:, None] * t[None, :])
    psi = np.stack(
        [(2.0 if n else 1.0) / nodes * (np.cos(n * theta) @ f) for n in range(NB)]
    )
    half = BL // 2
    ang = np.pi * np.outer(np.arange(BL), 2 * np.arange(half) + 1) / BL
    c, s = np.cos(ang), np.sin(ang)
    z = np.zeros_like(c)
    fwd = np.block([[c, z, -s, z], [z, c, z, -s]])
    inv = np.block([[c, z, -s, z], [z, c, z, -s]]).T * (2.0 / BL)
    spec = np.concatenate([psi[:, :BL] @ c] * 2 + [-psi[:, :BL] @ s] * 2, axis=1)
    unit = np.concatenate([np.ones((1, BL)), np.zeros((1, BL))], axis=1)
    spec = np.concatenate([spec, unit, np.zeros((15, 2 * BL))], axis=0)
    rev = psi[:, BL - 1 :: -1][:, :BL]
    zr = np.zeros_like(rev)
    mom = np.block([[rev, zr], [zr, rev]])
    nxt = psi[:, 1 : BL + 1]
    car = np.block([[nxt, zr], [zr, nxt]])
    sh, sl = split(spec)
    mh, ml = split(mom)
    ch, cl = split(car)
    sel = np.zeros((8, 6 * 128))
    for i in range(3):
        sel[2 * i + 1, (2 * i) * 128] = 1
        sel[2 * i, (2 * i + 1) * 128] = 1
        sel[2 * i + 1, (2 * i + 1) * 128 + 1] = 1
    wide = np.kron(np.eye(9), np.ones((1, 128)))
    wide = np.concatenate([wide, np.zeros((7, 9 * 128))], axis=0)
    wide = np.concatenate([wide, wide], axis=0)
    cat = lambda *a: np.concatenate(a, axis=0)
    b16 = lambda a: a.astype(jnp.bfloat16)
    return dict(
        fwd=b16(fwd), inv=b16(inv), spec=cat(sh, sh, sl), mom=cat(mh, ml),
        car=cat(ch, ch, cl), sel=b16(sel), wide=b16(wide),
    )


def rowdot(a, b):
    return lax.dot_general(a, b, (((0,), (0,)), ((), ())), preferred_element_type=jnp.float32)


def three(m):
    hi = m.astype(jnp.bfloat16)
    lo = (m - hi.astype(jnp.float32)).astype(jnp.bfloat16)
    return jnp.concatenate([hi, lo, hi], axis=0)


def dot(a, b):
    return jnp.dot(a, b, preferred_element_type=jnp.float32)


def two(m):
    hi = m.astype(jnp.bfloat16)
    lo = (m - hi.astype(jnp.float32)).astype(jnp.bfloat16)
    return jnp.concatenate([hi, lo], axis=0)


def padded(ref, count):
    parts = [ref[i].astype(jnp.float32) for i in range(3)]
    rest = count - 3 * ref.shape[1]
    return jnp.concatenate(parts + [jnp.zeros((rest, ref.shape[2]), jnp.float32)], axis=0)


def series(decay, cheb_ref):
    xi = decay * (1.0 / HALF) - 1.0
    a, b = jnp.ones_like(xi), xi
    for n in range(NB):
        cheb_ref[n * 16 : n * 16 + 16] = a
        a, b = b, 2.0 * xi * b - a


def feat(x, w_ref, rows, h1, h2, first):
    lane = lax.broadcasted_iota(jnp.int32, (x.shape[0], 128), 1)
    w0, w1, w2 = (w_ref[rows, (first + i) * 128 : (first + i + 1) * 128] for i in range(3))
    out = []
    for i in range(x.shape[1] // 128):
        c = x[:, i * 128 : (i + 1) * 128].astype(jnp.float32)
        r1, r2 = pltpu.roll(c, 1, 1), pltpu.roll(c, 2, 1)
        out.append(w0 * c + w1 * jnp.where(lane < 1, h1, r1) + w2 * jnp.where(lane < 2, h2, r2))
        h1, h2 = r1, r2
    return out


ROWS = 64


def front(p_ref, halo_ref, w_ref, decay_ref, sel_ref, wide_ref, mom_ref,
          mixed_ref, ends_ref, last_ref, power_ref,
          hr_ref, wide_w, cheb_ref):
    tile, length = p_ref.shape[1:]
    hr_ref[...] = rowdot(padded(halo_ref, 8).astype(jnp.bfloat16), sel_ref[:, 256:])
    wide_w[...] = rowdot(two(padded(w_ref, 16)), wide_ref[:, 384:])
    series(decay_ref[...], cheb_ref)

    @pl.loop(0, tile // ROWS)
    def _(r):
        rows = pl.ds(pl.multiple_of(r * ROWS, ROWS), ROWS)
        k = feat(p_ref[0, rows, :], wide_w, rows, hr_ref[rows, 0:128], hr_ref[rows, 128:256], 0)
        v = feat(p_ref[1, rows, :], wide_w, rows, hr_ref[rows, 256:384], hr_ref[rows, 384:512], 3)
        for i in range(len(k)):
            mixed_ref[rows, i * 128 : (i + 1) * 128] = (k[i] * v[i]).astype(jnp.bfloat16)

    step = jnp.exp(-BL * decay_ref[...])
    total = None
    for pair in range(length // 256):
        m = lax.dot_general(
            mom_ref[...], mixed_ref[:, pair * 256 : (pair + 1) * 256],
            (((1,), (1,)), ((), ())), preferred_element_type=jnp.float32)
        m = m[:32] + m[32:]
        for b in range(2):
            e = cheb_ref[0:16] * m[b * 16 : b * 16 + 1]
            for i in range(1, NB):
                e = e + cheb_ref[i * 16 : i * 16 + 16] * m[b * 16 + i : b * 16 + i + 1]
            ends_ref[(pair * 2 + b) * 16 : (pair * 2 + b + 1) * 16] = e
            total = e if total is None else step * total + e
    last_ref[...] = total.astype(last_ref.dtype)
    power_ref[...] = jnp.exp(-length * decay_ref[...])


def exchange(n, last_ref, power_ref, init_ref, peer, pair, inbox, give, got, send_sem, recv_sem, swap_send, swap_recv):
    me = lax.axis_index("seq")
    odd = lax.rem(me, 2)
    partner = me + 1 - 2 * odd
    half = last_ref.shape[1] // 2
    own = pl.ds(pl.multiple_of(odd * half, half), half)
    other = pl.ds(pl.multiple_of((1 - odd) * half, half), half)
    barrier = pltpu.get_barrier_semaphore()

    def greet(j):
        pl.semaphore_signal(barrier, inc=1, device_id={"seq": j}, device_id_type=pl.DeviceIdType.MESH)

    greet(partner)

    @pl.loop(0, n // 2)
    def _(i):
        @pl.when(2 * i + odd != me)
        def _():
            greet(2 * i + odd)

    pl.semaphore_wait(barrier, n // 2)

    def swap(src, dst, i):
        return pltpu.make_async_remote_copy(
            src_ref=src, dst_ref=dst, send_sem=swap_send.at[i], recv_sem=swap_recv.at[i],
            device_id={"seq": partner}, device_id_type=pl.DeviceIdType.MESH)

    def copy(i, source):
        return pltpu.make_async_remote_copy(
            src_ref=pair, dst_ref=inbox.at[source], send_sem=send_sem.at[i], recv_sem=recv_sem.at[source],
            device_id={"seq": 2 * i + odd}, device_id_type=pl.DeviceIdType.MESH)

    at = lax.div(me, 2)
    first = swap(last_ref.at[:, other], peer, 0)
    first.start()
    power = power_ref[:, own]
    mine = last_ref[:, own].astype(jnp.float32)
    first.wait_recv()
    theirs = peer[...].astype(jnp.float32)
    even = odd == 0
    e0 = jnp.where(even, mine, theirs)
    e1 = jnp.where(even, theirs, mine)
    pair[...] = (power * e0 + e1).astype(pair.dtype)

    @pl.loop(0, n // 2)
    def _(i):
        @pl.when(i > at)
        def _():
            copy(i, at).start()

    init_ref[:, own] = jnp.zeros((16, half), jnp.float32)

    @pl.loop(0, n // 2)
    def _(i):
        @pl.when(i < at)
        def _():
            copy(at, i).wait_recv()
            init_ref[:, own] = power * power * init_ref[:, own] + inbox[i].astype(jnp.float32)

    start = init_ref[:, own]
    later = power * start + e0
    give[...] = jnp.where(even, later, start).astype(give.dtype)
    second = swap(give, got, 1)
    second.start()
    init_ref[:, own] = jnp.where(even, start, later)
    second.wait_recv()
    init_ref[:, other] = got[...].astype(jnp.float32)
    first.wait_send()
    second.wait_send()

    @pl.loop(0, n // 2)
    def _(i):
        @pl.when(i > at)
        def _():
            copy(i, at).wait_send()


def back(q_ref, mixed_ref, halo_ref, w_ref, decay_ref, residue_ref, skip_ref, ends_ref, init_ref,
         sel_ref, wide_ref, fwd_ref, inv_ref, spec_ref, car_ref,
         out_ref, hr_ref, h_ref, y_ref, wide_w, cheb_ref):
    tile = mixed_ref.shape[0]
    hr_ref[...] = rowdot(padded(halo_ref, 8).astype(jnp.bfloat16), sel_ref[:, :256])
    wide_w[...] = rowdot(two(padded(w_ref, 16)), wide_ref[:, :384])
    series(decay_ref[...], cheb_ref)
    step = jnp.exp(-BL * decay_ref[...])
    fold = 1.0 / (1.0 + step)
    weight = residue_ref[...] * jnp.sqrt(2.0 * decay_ref[...])
    wv = weight * fold
    g = [jnp.sum(wv * cheb_ref[n * 16 : n * 16 + 16], axis=0, keepdims=True) for n in range(NB)]
    g = jnp.concatenate(g + [skip_ref[...], jnp.zeros((15, tile), jnp.float32)], axis=0)
    h_ref[...] = rowdot(three(g), spec_ref[...])
    state = init_ref[...]
    for pair in range(mixed_ref.shape[1] // 256):
        c = []
        for b in range(2):
            e = ends_ref[(pair * 2 + b) * 16 : (pair * 2 + b + 1) * 16]
            p = weight * (state + fold * e)
            state = step * state + e
            c += [jnp.sum(p * cheb_ref[n * 16 : n * 16 + 16], axis=0, keepdims=True) for n in range(NB)]
        cols = slice(pair * 256, pair * 256 + 256)
        carried = rowdot(three(jnp.concatenate(c, axis=0)), car_ref[...])
        x = dot(mixed_ref[:, cols], fwd_ref[...])
        xr, xi = x[:, :128], x[:, 128:]
        hr, hi = h_ref[:, :128], h_ref[:, 128:]
        y = jnp.concatenate([xr * hr - xi * hi, xr * hi + xi * hr], axis=1).astype(jnp.bfloat16)
        y_ref[:, cols] = (carried + dot(y, inv_ref[...])).astype(jnp.bfloat16)

    @pl.loop(0, tile // ROWS)
    def _(r):
        rows = pl.ds(pl.multiple_of(r * ROWS, ROWS), ROWS)
        q = feat(q_ref[0, rows, :], wide_w, rows, hr_ref[rows, 0:128], hr_ref[rows, 128:256], 0)
        for i in range(len(q)):
            cols = slice(i * 128, i * 128 + 128)
            out_ref[rows, cols] = (q[i] * y_ref[rows, cols].astype(jnp.float32)).astype(jnp.bfloat16)


def shards(projected, short_weight, skip_weight, decay_rates, residues):
    channels, length = projected.shape[1:]
    n = lax.axis_size("seq")
    tab = {k: jnp.asarray(v) for k, v in tables().items()}
    tile = math.gcd(512, channels)
    blocks = length // BL
    taps = jnp.swapaxes(short_weight, 1, 2)
    tail = jnp.swapaxes(projected[:, :, length - 2 :], 1, 2)
    halo = lax.ppermute(tail, "seq", [(i, i + 1) for i in range(n - 1)])
    decay, residue = decay_rates.T, residues.T

    streams = lambda r: pl.BlockSpec((3, r, tile), lambda i: (0, 0, i))
    full = lambda a: pl.BlockSpec(a.shape, lambda i: (0,) * a.ndim)
    lanes = lambda r: pl.BlockSpec((r, tile), lambda i: (0, i))
    rows = pl.BlockSpec((tile, length), lambda i: (i, 0))
    limit = 56 * 2**20
    count = channels // tile
    names = ("sel", "wide", "mom")
    mixed, ends, last, power = pl.pallas_call(
        front,
        grid=(count,),
        in_specs=[pl.BlockSpec((pl.Element(2), pl.Element(tile), pl.Element(length)), lambda i: (1, i * tile, 0)),
                  streams(2), streams(3), lanes(16)] + [full(tab[k]) for k in names],
        out_specs=[rows, lanes(blocks * 16), lanes(16), lanes(16)],
        out_shape=[
            jax.ShapeDtypeStruct((channels, length), jnp.bfloat16),
            jax.ShapeDtypeStruct((blocks * 16, channels), jnp.float32),
            jax.ShapeDtypeStruct((16, channels), jnp.bfloat16),
            jax.ShapeDtypeStruct((16, channels), jnp.float32),
        ],
        scratch_shapes=[
            pltpu.VMEM((tile, 512), jnp.float32),
            pltpu.VMEM((tile, 6 * 128), jnp.float32),
            pltpu.VMEM((NB * 16, tile), jnp.float32),
        ],
        compiler_params=pltpu.CompilerParams(vmem_limit_bytes=limit),
        name="front",
    )(projected, halo, taps, decay, *[tab[k] for k in names])
    init = pl.pallas_call(
        functools.partial(exchange, n),
        in_specs=[pl.BlockSpec(memory_space=pltpu.VMEM)] * 2,
        out_specs=pl.BlockSpec(memory_space=pltpu.VMEM),
        out_shape=jax.ShapeDtypeStruct((16, channels), jnp.float32),
        scratch_shapes=[
            pltpu.VMEM((16, channels // 2), jnp.bfloat16),
            pltpu.VMEM((16, channels // 2), jnp.bfloat16),
            pltpu.VMEM((n // 2, 16, channels // 2), jnp.bfloat16),
            pltpu.VMEM((16, channels // 2), jnp.bfloat16),
            pltpu.VMEM((16, channels // 2), jnp.bfloat16),
            pltpu.SemaphoreType.DMA((n // 2,)),
            pltpu.SemaphoreType.DMA((n // 2,)),
            pltpu.SemaphoreType.DMA((2,)),
            pltpu.SemaphoreType.DMA((2,)),
        ],
        compiler_params=pltpu.CompilerParams(collective_id=0, has_side_effects=True),
        name="exchange",
    )(last, power)
    names = ("sel", "wide", "fwd", "inv", "spec", "car")
    return pl.pallas_call(
        back,
        grid=(count,),
        in_specs=[pl.BlockSpec((1, tile, length), lambda i: (0, i, 0)), rows, streams(2), streams(3), lanes(16),
                  lanes(16), lanes(1), lanes(blocks * 16), lanes(16)] + [full(tab[k]) for k in names],
        out_specs=rows,
        out_shape=jax.ShapeDtypeStruct((channels, length), jnp.bfloat16),
        scratch_shapes=[
            pltpu.VMEM((tile, 256), jnp.float32),
            pltpu.VMEM((tile, 256), jnp.float32),
            pltpu.VMEM((tile, length), jnp.bfloat16),
            pltpu.VMEM((tile, 3 * 128), jnp.float32),
            pltpu.VMEM((NB * 16, tile), jnp.float32),
        ],
        compiler_params=pltpu.CompilerParams(vmem_limit_bytes=limit),
        name="back",
    )(projected, mixed, halo, taps, decay, residue, skip_weight[None], ends, init, *[tab[k] for k in names])


def solution(mesh):
    return jax.shard_map(
        shards,
        mesh=mesh,
        in_specs=(
            P(None, "fsdp", "seq"),
            P(None, "fsdp", None),
            P("fsdp"),
            P("fsdp", None),
            P("fsdp", None),
        ),
        out_specs=P("fsdp", "seq"),
        check_vma=False,
    )
```
